256 devices in a mesh: half: 2 (over z_hi), bf: 128 (over z_lo, y, x, core).
Axes of the slice: x: 4, y: 4, z: 8 (z_hi: 2, z_lo: 4; z = z_hi * 4 + z_lo), core: 2. Of those that a mesh axis runs over, the one named last changes fastest.
Arguments:
- sources: float32 [2, 32, 1048576], P(None, None, ('half', 'bf')), may hold values from -6 to 6
- coarse_in: bfloat16 [2, 4096, 64, 256], P(None, ('half', 'bf')), may hold values from -0.25 to 0.25
- coarse_mix_in: bfloat16 [2, 256, 1024, 512], P(None, ('half', 'bf')), may hold values from -0.125 to 0.125
- coarse_mix_out: bfloat16 [2, 256, 512, 1024], P(None, ('half', 'bf')), may hold values from -0.1875 to 0.1875
- coarse_out: bfloat16 [2, 4096, 64, 256], P(None, ('half', 'bf')), may hold values from -0.5 to 0.5
- fine_in: bfloat16 [2, 4096, 64, 256], P(None, ('half', 'bf')), may hold values from -0.25 to 0.25
- fine_mix_in: bfloat16 [2, 256, 2, 512, 256], P(None, ('half', 'bf')), may hold values from -0.1875 to 0.1875
- fine_mix_out: bfloat16 [2, 256, 2, 256, 512], P(None, ('half', 'bf')), may hold values from -0.25 to 0.25
- fine_out: bfloat16 [2, 4096, 64, 256], P(None, ('half', 'bf')), may hold values from -0.5 to 0.5
- ranks: int32 [4, 4096], P(None, ('half', 'bf')), may hold values from 16 to 64, as said below
Outputs:
- product: float32 [2, 32, 1048576], P(None, None, ('half', 'bf'))
The draws below stay inside these ranges and needn't reach their ends.
Inputs may be any that keep to these rules, and one draw needn't show every extreme that they name: Each of the four rows of ranks reaches both ends of the range.
All inputs are finite; a program needn't handle non-finite values.
Results may differ from the reference program's by a relative error of at most 0.0057.
Values may be sent and summed in bfloat16 or wider, within the bound.
A program may use at most 64 MiB of HBM per device.

```python
from functools import partial
import jax
import jax.numpy as jnp
from jax import lax

ROWS_DEV = 4096
VECTORS = 32
LEAF = 256
RANK = 64
LINKS = 4
FINE_LINKS = 2
LEAF_DEV = 16
GROUPS = 128
LEAVES = 4096
ORDER = 1048576


def draw_ranks(key, part):
    key = jax.random.fold_in(key, 7)
    values = jax.random.randint(key, (4, LEAVES), RANK // 4, RANK + 1, dtype=jnp.int32)
    values = values.at[:, 0].set(RANK)
    values = values.at[:, 1].set(RANK // 4)
    return values


def steps_of(stream_key, extent, split, smallest, top_value):
    def one(axis_at, parts):
        draws = jax.random.uniform(jax.random.fold_in(jax.random.fold_in(stream_key, 6), axis_at), (parts,), jnp.float32, smallest / len(split), top_value / len(split))
        return jnp.repeat(jnp.exp(draws), extent[axis_at] // parts).reshape((-1,) + (1,) * (len(extent) - axis_at - 1))

    level = one(*split[0])
    for cut in split[1:]:
        level = level * one(*cut)
    return level


def noise(key, dims, scale, most, split=(), kind=jnp.bfloat16):
    gain = steps_of(key, dims, split, -0.22, 0.18) if split else 1.0
    values = jax.random.normal(key, dims, jnp.float32) * scale * gain
    return jnp.minimum(jnp.maximum(values, -most), most).astype(kind)


def setup_inputs(seed: int = 0) -> dict:
    keys = jax.random.split(jax.random.key(seed), 11)
    return {
        "sources": noise(keys[0], (2, VECTORS, ORDER), 1.0, 6.0, ((2, 256),), jnp.float32),
        "coarse_in": noise(keys[1], (2, LEAVES, RANK, LEAF), (2 * LEAF) ** -0.5, 0.25, ((1, 256),)),
        "coarse_mix_in": noise(keys[2], (2, 2 * GROUPS, LEAF_DEV * RANK, GROUPS * LINKS), (2 * LEAF_DEV * RANK) ** -0.5, 0.125, ((1, 256),)),
        "coarse_mix_out": noise(keys[3], (2, 2 * GROUPS, GROUPS * LINKS, LEAF_DEV * RANK), (2 * GROUPS * LINKS) ** -0.5, 0.1875, ((1, 256),)),
        "coarse_out": noise(keys[4], (2, LEAVES, RANK, LEAF), (2 * RANK) ** -0.5, 0.5, ((1, 256),)),
        "fine_in": noise(keys[5], (2, LEAVES, RANK, LEAF), (2 * LEAF) ** -0.5, 0.25, ((1, 256),)),
        "fine_mix_in": noise(keys[6], (2, 2 * GROUPS, 2, LEAF_DEV // 2 * RANK, GROUPS * FINE_LINKS), (LEAF_DEV * RANK) ** -0.5, 0.1875, ((1, 256),)),
        "fine_mix_out": noise(keys[7], (2, 2 * GROUPS, 2, GROUPS * FINE_LINKS, LEAF_DEV // 2 * RANK), (2 * GROUPS * FINE_LINKS) ** -0.5, 0.25, ((1, 256),)),
        "fine_out": noise(keys[8], (2, LEAVES, RANK, LEAF), (2 * RANK) ** -0.5, 0.5, ((1, 256),)),
        "ranks": draw_ranks(jax.random.fold_in(keys[10], 71), 0),
    }


def cmul(spec, left, right):
    first = left.astype(jnp.float32)
    second = right.astype(jnp.float32)
    contract = partial(jnp.einsum, spec, precision=lax.Precision.HIGHEST)
    real_part = contract(first[0], second[0]) - contract(first[1], second[1])
    imag_part = contract(first[0], second[1]) + contract(first[1], second[0])
    return jnp.stack([real_part, imag_part])


def reference(sources, coarse_in, coarse_mix_in, coarse_mix_out, coarse_out, fine_in, fine_mix_in, fine_mix_out, fine_out, ranks):
    blocks = 2 * GROUPS
    halfway = LEAF_DEV // 2

    def regroup(array):
        return jnp.moveaxis(array.reshape((2, blocks) + array.shape[2:]), 1, 0)

    def leafwise(array):
        return jnp.moveaxis(array.reshape(2, blocks, LEAF_DEV, RANK, LEAF), 1, 0)

    narrow = sources.astype(jnp.bfloat16).reshape(2, VECTORS, blocks, LEAF_DEV, LEAF).transpose(2, 0, 1, 3, 4)
    keeper = (jnp.arange(RANK)[None, None, :] < ranks[:, :, None]).astype(jnp.float32)
    keeper = keeper.reshape(4, blocks, LEAF_DEV, RANK).transpose(1, 0, 2, 3)

    def column_block(items):
        block_x, c_in, c_mix, f_in, f_mix, keep = items
        coarse_coef = (cmul('nsl,skl->nsk', block_x, c_in) * keep[0]).astype(jnp.bfloat16)
        coarse_send = cmul('nk,kj->nj', coarse_coef.reshape(2, VECTORS, LEAF_DEV * RANK), c_mix).astype(jnp.bfloat16)
        fine_coef = (cmul('nsl,skl->nsk', block_x, f_in) * keep[2]).astype(jnp.bfloat16)
        fine_send = cmul('njk,jkm->njm', fine_coef.reshape(2, VECTORS, 2, halfway * RANK), f_mix).astype(jnp.bfloat16)
        return coarse_send, fine_send

    coarse_send, fine_send = lax.map(column_block, (narrow, leafwise(coarse_in), regroup(coarse_mix_in), leafwise(fine_in), regroup(fine_mix_in), keeper))
    coarse_recv = jnp.flip(coarse_send.reshape(2, GROUPS, 2, VECTORS, GROUPS, LINKS), 0)
    coarse_recv = coarse_recv.transpose(0, 4, 2, 3, 1, 5).reshape(blocks, 2, VECTORS, GROUPS * LINKS)
    fine_recv = fine_send.reshape(2, GROUPS, 2, VECTORS, 2, GROUPS, FINE_LINKS)
    fine_recv = fine_recv.transpose(0, 5, 2, 3, 4, 1, 6).reshape(blocks, 2, VECTORS, 2, GROUPS * FINE_LINKS)

    def row_block(items):
        c_recv, f_recv, c_mix, c_out, f_mix, f_out, keep = items
        coarse_back = cmul('nj,jk->nk', c_recv, c_mix).reshape(2, VECTORS, LEAF_DEV, RANK)
        coarse_back = (coarse_back * keep[1]).astype(jnp.bfloat16)
        coarse_part = cmul('nsk,skl->nsl', coarse_back, c_out)
        fine_back = cmul('njm,jmk->njk', f_recv, f_mix)
        fine_back = jnp.flip(fine_back, 2).reshape(2, VECTORS, LEAF_DEV, RANK)
        fine_back = (fine_back * keep[3]).astype(jnp.bfloat16)
        fine_part = cmul('nsk,skl->nsl', fine_back, f_out)
        return (coarse_part + fine_part).reshape(2, VECTORS, ROWS_DEV)

    rows = lax.map(row_block, (coarse_recv, fine_recv, regroup(coarse_mix_out), leafwise(coarse_out), regroup(fine_mix_out), leafwise(fine_out), keeper))
    return rows.transpose(1, 2, 0, 3).reshape(2, VECTORS, ORDER)
```

```python
import functools

import jax
import jax.numpy as jnp
from jax import lax
from jax.experimental import pallas as pl
from jax.experimental.pallas import tpu as pltpu
from jax.sharding import PartitionSpec as P

F32 = jnp.float32
BF16 = jnp.bfloat16
MESH = pl.DeviceIdType.MESH
GROUPS = 8
MEMBERS = 16
ROWS = 32
LEAVES = 16
RANK = 64
LEAF = 256
VECTORS = 32
CHUNKS = 4


def dot(left, right):
    return lax.dot_general(left, right, (((1,), (0,)), ((), ())), preferred_element_type=F32)


def dot_t(left, right):
    return lax.dot_general(left, right, (((1,), (1,)), ((), ())), preferred_element_type=F32)


def iota(shape, axis):
    return lax.broadcasted_iota(jnp.int32, shape, axis)


def complex_rows(by_real, by_imag):
    n = VECTORS
    return by_real[:n] - by_imag[n:], by_real[n:] + by_imag[:n]


def kernel(
    sources, coarse_in, coarse_mix_in, coarse_mix_out, coarse_out,
    fine_in, fine_mix_in, fine_mix_out, fine_out, ranks,
    out,
    x_v, ci_v, cmi_v, cmo_v, co_v, fi_v, fmi_v, fmo_v, fo_v, ranks_s,
    regroup, pairs, spread, ccoef, fcoef, cback, fback,
    cs1, cr1, cs2, cr2, fs1, fr1, fs2, fr2, out_v,
    in_sem, send_sem, recv_sem, out_sem,
):
    half = lax.axis_index("half")
    block = lax.axis_index("bf")
    group = block // MEMBERS
    member = block % MEMBERS

    per = LEAVES // CHUNKS
    loads = {}

    def load(name, source, target):
        copy = pltpu.make_async_copy(source, target, in_sem.at[len(loads)])
        copy.start()
        loads[name] = copy

    load("ranks", ranks, ranks_s)
    for c in range(CHUNKS):
        span = pl.ds(c * per, per)
        cols = pl.ds(c * per * LEAF, per * LEAF)
        load(("x", c), sources.at[:, :, cols], x_v.at[:, :, cols])
        load(("ci", c), coarse_in.at[:, span], ci_v.at[:, span])
        load(("fi", c), fine_in.at[:, span], fi_v.at[:, span])
    load("cmi", coarse_mix_in, cmi_v)
    load("fmi", fine_mix_in, fmi_v)
    load("cmo", coarse_mix_out, cmo_v)
    load("fmo", fine_mix_out, fmo_v)
    load("co", coarse_out, co_v)
    load("fo", fine_out, fo_v)

    barrier = pltpu.get_barrier_semaphore()

    def greet(h, b):
        pl.semaphore_signal(barrier, inc=1, device_id=(h, b), device_id_type=MESH)

    for k in range(GROUPS):
        there = (group + k) % GROUPS * MEMBERS + member
        greet(1 - half, there)
        if k:
            greet(half, there)
    for k in range(1, MEMBERS):
        greet(half, group * MEMBERS + (member + k) % MEMBERS)

    def regrouped(row):
        return row // 2 % GROUPS * ROWS + row // (2 * GROUPS) * 2 + row % 2

    rows = iota((256, 256), 0)
    regroup[...] = (regrouped(rows) == iota((256, 256), 1)).astype(F32).astype(BF16)
    rows = iota((256, 512), 0)
    cols = iota((256, 512), 1) // 2
    spread[...] = (regrouped(rows) == cols).astype(F32).astype(BF16)
    pairs[...] = (rows == cols).astype(F32).astype(BF16)

    lane = iota((1, 128), 1)
    low = lane < RANK

    def keep(first, second):
        return lane < jnp.where(low, first, second + RANK)

    loads["ranks"].wait()
    for c in range(CHUNKS):
        for name in ("x", "ci", "fi"):
            loads[name, c].wait()
        for first in range(c * per, (c + 1) * per, 2):
            got = []
            for s in (first, first + 1):
                x = x_v[:, :, s * LEAF : (s + 1) * LEAF].astype(BF16).reshape(2 * VECTORS, LEAF)
                two = (ci_v, fi_v) if s == first else (fi_v, ci_v)
                w = jnp.concatenate([two[0][0, s], two[1][0, s], two[0][1, s], two[1][1, s]], axis=0)
                y = dot_t(x, w)
                re, im = complex_rows(y[:, :128], y[:, 128:])
                which = (0, 2) if s == first else (2, 0)
                kept = keep(ranks_s[which[0], s], ranks_s[which[1], s])
                both = jnp.concatenate([re, im], axis=0)
                got.append(jnp.where(kept, both, 0.0))
            at = pl.ds(first * RANK, 2 * RANK)
            ccoef[:, at] = jnp.where(low, got[0], got[1]).astype(BF16)
            fcoef[:, at] = jnp.where(low, got[1], got[0]).astype(BF16)

    def remote(source, target, which, h, b):
        pltpu.make_async_remote_copy(
            src_ref=source, dst_ref=target, send_sem=send_sem.at[which], recv_sem=recv_sem.at[which],
            device_id=(h, b), device_id_type=MESH,
        ).start()

    def arrived(buffer, which):
        pltpu.make_async_copy(buffer, buffer, recv_sem.at[which]).wait()

    def sent(buffer, which):
        pltpu.make_async_copy(buffer, buffer, send_sem.at[which]).wait()

    loads["cmi"].wait()
    re, im = complex_rows(dot(ccoef[...], cmi_v[0, 0]), dot(ccoef[...], cmi_v[1, 0]))
    send = jnp.concatenate([re, im], axis=0)
    even = iota((1, 512), 1) % 2 == 0
    send = jnp.concatenate([jnp.where(even, send, 0.0), jnp.where(even, 0.0, send)], axis=0).astype(BF16)
    cs1[...] = dot_t(pairs[...], send).astype(BF16).reshape(GROUPS, ROWS, 128)

    pl.semaphore_wait(barrier, 2 * GROUPS - 1 + MEMBERS - 1)
    for k in range(GROUPS):
        there = (group + k) % GROUPS
        remote(cs1.at[there], cr1.at[group], 0, 1 - half, there * MEMBERS + member)

    loads["fmi"].wait()
    fine = []
    for i in range(2):
        left = fcoef[:, i * 512 : (i + 1) * 512]
        parts = []
        for part in range(2):
            order = [leaf ^ 1 for leaf in range(LEAVES // 2)]
            w = jnp.concatenate(
                [fmi_v[part, 0, i, leaf * RANK : (leaf + 1) * RANK, :] for leaf in order], axis=0
            )
            parts.append(dot(left, w))
        fine.extend(complex_rows(*parts))
    send = jnp.concatenate(fine, axis=0)
    fs1[...] = send.T.astype(BF16).reshape(GROUPS, ROWS, 128)
    for k in range(1, GROUPS):
        there = (group + k) % GROUPS
        remote(fs1.at[there], fr1.at[group], 1, half, there * MEMBERS + member)
    pltpu.make_async_copy(fs1.at[group], fr1.at[group], recv_sem.at[1]).start()

    def pass_on(received, outgoing, landing, first, which):
        arrived(received, first)
        rows = received[...].reshape(256, 128)
        outgoing[...] = dot(regroup[...], rows).astype(BF16).reshape(MEMBERS, 2 * GROUPS, 128)
        for k in range(1, MEMBERS):
            there = (member + k) % MEMBERS
            remote(outgoing.at[there], landing.at[member], which, half, group * MEMBERS + there)
        pltpu.make_async_copy(outgoing.at[member], landing.at[member], recv_sem.at[which]).start()

    pass_on(cr1, cs2, cr2, 0, 2)
    pass_on(fr1, fs2, fr2, 1, 3)

    arrived(cr2, 2)
    got = dot(cr2[...].reshape(256, 128).T, spread[...])
    left = jnp.where(even, got[:64], got[64:]).astype(BF16)
    loads["cmo"].wait()
    for at in range(0, 1024, 256):
        re, im = complex_rows(dot(left, cmo_v[0, 0, :, at : at + 256]), dot(left, cmo_v[1, 0, :, at : at + 256]))
        for n in range(2):
            leaf = at // RANK + 2 * n
            kept = keep(ranks_s[1, leaf], ranks_s[1, leaf + 1])
            cols = slice(128 * n, 128 * n + 128)
            cback[0, :, at + 128 * n : at + 128 * n + 128] = jnp.where(kept, re[:, cols], 0.0)
            cback[1, :, at + 128 * n : at + 128 * n + 128] = jnp.where(kept, im[:, cols], 0.0)

    arrived(fr2, 3)
    got = dot(fr2[...].reshape(256, 128).T, regroup[...]).astype(BF16)
    loads["fmo"].wait()
    for i in range(2):
        left = got[i * 64 : i * 64 + 64]
        for at in range(0, 512, 256):
            re, im = complex_rows(
                dot(left, fmo_v[0, 0, i, :, at : at + 256]), dot(left, fmo_v[1, 0, i, :, at : at + 256])
            )
            for n in range(2):
                place = (1 - i) * 512 + at + 128 * n
                leaf = place // RANK
                kept = keep(ranks_s[3, leaf], ranks_s[3, leaf + 1])
                cols = slice(128 * n, 128 * n + 128)
                fback[0, :, place : place + 128] = pltpu.roll(jnp.where(kept, re[:, cols], 0.0), RANK, 1)
                fback[1, :, place : place + 128] = pltpu.roll(jnp.where(kept, im[:, cols], 0.0), RANK, 1)

    loads["co"].wait()
    loads["fo"].wait()
    for first in range(0, LEAVES, 2):
        at = slice(first * RANK, first * RANK + 128)
        cr, ci, fr, fi = cback[0, :, at], cback[1, :, at], fback[0, :, at], fback[1, :, at]
        for s in (first, first + 1):
            if s == first:
                re, im = jnp.where(low, cr, fr), jnp.where(low, ci, fi)
                two = (co_v, fo_v)
            else:
                re, im = jnp.where(low, fr, cr), jnp.where(low, fi, ci)
                two = (fo_v, co_v)
            left = jnp.concatenate(
                [jnp.concatenate([re, -im], axis=1), jnp.concatenate([im, re], axis=1)], axis=0
            ).astype(BF16)
            w = jnp.concatenate([two[0][0, s], two[1][0, s], two[0][1, s], two[1][1, s]], axis=0)
            out_v[:, :, s * LEAF : (s + 1) * LEAF] = dot(left, w).reshape(2, VECTORS, LEAF)
        if first % per == per - 2:
            span = pl.ds((first + 2 - per) * LEAF, per * LEAF)
            pltpu.make_async_copy(out_v.at[:, :, span], out.at[:, :, span], out_sem.at[first // per]).start()

    sent(cs1, 0)
    sent(fs1.at[pl.ds(0, GROUPS - 1)], 1)
    sent(cs2.at[pl.ds(0, MEMBERS - 1)], 2)
    sent(fs2.at[pl.ds(0, MEMBERS - 1)], 3)
    for c in range(CHUNKS):
        span = pl.ds(c * per * LEAF, per * LEAF)
        pltpu.make_async_copy(out_v.at[:, :, span], out.at[:, :, span], out_sem.at[c]).wait()


def local(*args):
    anywhere = pl.BlockSpec(memory_space=pl.ANY)
    shapes = [a.shape for a in args]
    vmem = pltpu.VMEM
    return pl.pallas_call(
        kernel,
        out_shape=jax.ShapeDtypeStruct(shapes[0], F32),
        in_specs=[anywhere] * len(args),
        out_specs=anywhere,
        scratch_shapes=[
            vmem(shapes[0], F32),
            *[vmem(s, BF16) for s in shapes[1:9]],
            pltpu.SMEM(shapes[9], jnp.int32),
            vmem((256, 256), BF16),
            vmem((256, 512), BF16),
            vmem((256, 512), BF16),
            vmem((64, 1024), BF16),
            vmem((64, 1024), BF16),
            vmem((2, 32, 1024), F32),
            vmem((2, 32, 1024), F32),
            *[
                vmem(s, BF16)
                for s in [
                    (GROUPS, ROWS, 128), (GROUPS, ROWS, 128), (MEMBERS, 2 * GROUPS, 128), (MEMBERS, 2 * GROUPS, 128),
                ]
                * 2
            ],
            vmem(shapes[0], F32),
            pltpu.SemaphoreType.DMA((1 + 3 * CHUNKS + 6,)),
            pltpu.SemaphoreType.DMA((4,)),
            pltpu.SemaphoreType.DMA((4,)),
            pltpu.SemaphoreType.DMA((CHUNKS,)),
        ],
        compiler_params=pltpu.CompilerParams(
            collective_id=0, has_side_effects=True, vmem_limit_bytes=40 * 1024 * 1024
        ),
        cost_estimate=pl.CostEstimate(flops=672 * 10**6, bytes_accessed=12 * 2**20, transcendentals=0),
    )(*args)


def solution(mesh):
    return jax.shard_map(
        local,
        mesh=mesh,
        in_specs=(
            P(None, None, ("half", "bf")),
            P(None, ("half", "bf"), None, None),
            P(None, ("half", "bf"), None, None),
            P(None, ("half", "bf"), None, None),
            P(None, ("half", "bf"), None, None),
            P(None, ("half", "bf"), None, None),
            P(None, ("half", "bf"), None, None, None),
            P(None, ("half", "bf"), None, None, None),
            P(None, ("half", "bf"), None, None),
            P(None, ("half", "bf")),
        ),
        out_specs=P(None, None, ("half", "bf")),
        check_vma=False,
    )
```

```python
import functools

import jax
import jax.numpy as jnp
from jax import lax
from jax.experimental import pallas as pl
from jax.experimental.pallas import tpu as pltpu
from jax.sharding import PartitionSpec as P

F32 = jnp.float32
BF16 = jnp.bfloat16
MESH = pl.DeviceIdType.MESH
GROUPS = 8
MEMBERS = 16
ROWS = 32
LEAVES = 16
RANK = 64
LEAF = 256
VECTORS = 32
CHUNKS = 4


def dot(left, right):
    return lax.dot_general(left, right, (((1,), (0,)), ((), ())), preferred_element_type=F32)


def dot_t(left, right):
    return lax.dot_general(left, right, (((1,), (1,)), ((), ())), preferred_element_type=F32)


def iota(shape, axis):
    return lax.broadcasted_iota(jnp.int32, shape, axis)


def complex_rows(by_real, by_imag):
    n = VECTORS
    return by_real[:n] - by_imag[n:], by_real[n:] + by_imag[:n]


def kernel(
    sources, coarse_in, coarse_mix_in, coarse_mix_out, coarse_out,
    fine_in, fine_mix_in, fine_mix_out, fine_out, ranks,
    out,
    x_v, ci_v, cmi_v, cmo_v, co_v, fi_v, fmi_v, fmo_v, fo_v, ranks_s,
    regroup, pairs, spread, ccoef, fcoef, cback, fback,
    cs1, cr1, cs2, cr2, fs1, fr1, fs2, fr2,
    in_sem, send_sem, recv_sem,
):
    half = lax.axis_index("half")
    block = lax.axis_index("bf")
    group = block // MEMBERS
    member = block % MEMBERS

    per = LEAVES // CHUNKS
    loads = {}

    def load(name, source, target):
        copy = pltpu.make_async_copy(source, target, in_sem.at[len(loads)])
        copy.start()
        loads[name] = copy

    load("ranks", ranks, ranks_s)
    for c in range(CHUNKS):
        span = pl.ds(c * per, per)
        cols = pl.ds(c * per * LEAF, per * LEAF)
        load(("x", c), sources.at[:, :, cols], x_v.at[:, :, cols])
        load(("ci", c), coarse_in.at[:, span], ci_v.at[:, span])
        load(("fi", c), fine_in.at[:, span], fi_v.at[:, span])
    load("cmi", coarse_mix_in, cmi_v)
    load("fmi", fine_mix_in, fmi_v)
    load("cmo", coarse_mix_out, cmo_v)
    load("fmo", fine_mix_out, fmo_v)
    load("co", coarse_out, co_v)
    load("fo", fine_out, fo_v)

    barrier = pltpu.get_barrier_semaphore()

    def greet(h, b):
        pl.semaphore_signal(barrier, inc=1, device_id=(h, b), device_id_type=MESH)

    for k in range(GROUPS):
        there = (group + k) % GROUPS * MEMBERS + member
        greet(1 - half, there)
        if k:
            greet(half, there)
    for k in range(1, MEMBERS):
        greet(half, group * MEMBERS + (member + k) % MEMBERS)

    def regrouped(row):
        return row // 2 % GROUPS * ROWS + row // (2 * GROUPS) * 2 + row % 2

    rows = iota((256, 256), 0)
    regroup[...] = (regrouped(rows) == iota((256, 256), 1)).astype(F32).astype(BF16)
    rows = iota((256, 512), 0)
    cols = iota((256, 512), 1) // 2
    spread[...] = (regrouped(rows) == cols).astype(F32).astype(BF16)
    pairs[...] = (rows == cols).astype(F32).astype(BF16)

    lane = iota((1, 128), 1)
    low = lane < RANK

    def keep(first, second):
        return lane < jnp.where(low, first, second + RANK)

    loads["ranks"].wait()
    for c in range(CHUNKS):
        for name in ("x", "ci", "fi"):
            loads[name, c].wait()
        for first in range(c * per, (c + 1) * per, 2):
            got = []
            for s in (first, first + 1):
                x = x_v[:, :, s * LEAF : (s + 1) * LEAF].astype(BF16).reshape(2 * VECTORS, LEAF)
                two = (ci_v, fi_v) if s == first else (fi_v, ci_v)
                w = jnp.concatenate([two[0][0, s], two[1][0, s], two[0][1, s], two[1][1, s]], axis=0)
                y = dot_t(x, w)
                re, im = complex_rows(y[:, :128], y[:, 128:])
                which = (0, 2) if s == first else (2, 0)
                kept = keep(ranks_s[which[0], s], ranks_s[which[1], s])
                both = jnp.concatenate([re, im], axis=0)
                got.append(jnp.where(kept, both, 0.0))
            at = pl.ds(first * RANK, 2 * RANK)
            ccoef[:, at] = jnp.where(low, got[0], got[1]).astype(BF16)
            fcoef[:, at] = jnp.where(low, got[1], got[0]).astype(BF16)

    def remote(source, target, which, h, b):
        pltpu.make_async_remote_copy(
            src_ref=source, dst_ref=target, send_sem=send_sem.at[which], recv_sem=recv_sem.at[which],
            device_id=(h, b), device_id_type=MESH,
        ).start()

    def arrived(buffer, which):
        pltpu.make_async_copy(buffer, buffer, recv_sem.at[which]).wait()

    def sent(buffer, which):
        pltpu.make_async_copy(buffer, buffer, send_sem.at[which]).wait()

    loads["cmi"].wait()
    re, im = complex_rows(dot(ccoef[...], cmi_v[0, 0]), dot(ccoef[...], cmi_v[1, 0]))
    send = jnp.concatenate([re, im], axis=0)
    even = iota((1, 512), 1) % 2 == 0
    send = jnp.concatenate([jnp.where(even, send, 0.0), jnp.where(even, 0.0, send)], axis=0).astype(BF16)
    cs1[...] = dot_t(pairs[...], send).astype(BF16).reshape(GROUPS, ROWS, 128)

    pl.semaphore_wait(barrier, 2 * GROUPS - 1 + MEMBERS - 1)
    for k in range(GROUPS):
        there = (group + k) % GROUPS
        remote(cs1.at[there], cr1.at[group], 0, 1 - half, there * MEMBERS + member)

    loads["fmi"].wait()
    fine = []
    for i in range(2):
        left = fcoef[:, i * 512 : (i + 1) * 512]
        parts = []
        for part in range(2):
            order = [leaf ^ 1 for leaf in range(LEAVES // 2)]
            w = jnp.concatenate(
                [fmi_v[part, 0, i, leaf * RANK : (leaf + 1) * RANK, :] for leaf in order], axis=0
            )
            parts.append(dot(left, w))
        fine.extend(complex_rows(*parts))
    send = jnp.concatenate(fine, axis=0)
    fs1[...] = send.T.astype(BF16).reshape(GROUPS, ROWS, 128)
    for k in range(1, GROUPS):
        there = (group + k) % GROUPS
        remote(fs1.at[there], fr1.at[group], 1, half, there * MEMBERS + member)
    pltpu.make_async_copy(fs1.at[group], fr1.at[group], recv_sem.at[1]).start()

    def pass_on(received, outgoing, landing, first, which):
        arrived(received, first)
        rows = received[...].reshape(256, 128)
        outgoing[...] = dot(regroup[...], rows).astype(BF16).reshape(MEMBERS, 2 * GROUPS, 128)
        for k in range(1, MEMBERS):
            there = (member + k) % MEMBERS
            remote(outgoing.at[there], landing.at[member], which, half, group * MEMBERS + there)
        pltpu.make_async_copy(outgoing.at[member], landing.at[member], recv_sem.at[which]).start()

    pass_on(cr1, cs2, cr2, 0, 2)
    pass_on(fr1, fs2, fr2, 1, 3)

    arrived(cr2, 2)
    got = dot(cr2[...].reshape(256, 128).T, spread[...])
    left = jnp.where(even, got[:64], got[64:]).astype(BF16)
    loads["cmo"].wait()
    for at in range(0, 1024, 256):
        re, im = complex_rows(dot(left, cmo_v[0, 0, :, at : at + 256]), dot(left, cmo_v[1, 0, :, at : at + 256]))
        for n in range(2):
            leaf = at // RANK + 2 * n
            kept = keep(ranks_s[1, leaf], ranks_s[1, leaf + 1])
            cols = slice(128 * n, 128 * n + 128)
            cback[0, :, at + 128 * n : at + 128 * n + 128] = jnp.where(kept, re[:, cols], 0.0)
            cback[1, :, at + 128 * n : at + 128 * n + 128] = jnp.where(kept, im[:, cols], 0.0)

    arrived(fr2, 3)
    got = dot(fr2[...].reshape(256, 128).T, regroup[...]).astype(BF16)
    loads["fmo"].wait()
    for i in range(2):
        left = got[i * 64 : i * 64 + 64]
        for at in range(0, 512, 256):
            re, im = complex_rows(
                dot(left, fmo_v[0, 0, i, :, at : at + 256]), dot(left, fmo_v[1, 0, i, :, at : at + 256])
            )
            for n in range(2):
                place = (1 - i) * 512 + at + 128 * n
                leaf = place // RANK
                kept = keep(ranks_s[3, leaf], ranks_s[3, leaf + 1])
                cols = slice(128 * n, 128 * n + 128)
                fback[0, :, place : place + 128] = pltpu.roll(jnp.where(kept, re[:, cols], 0.0), RANK, 1)
                fback[1, :, place : place + 128] = pltpu.roll(jnp.where(kept, im[:, cols], 0.0), RANK, 1)

    loads["co"].wait()
    loads["fo"].wait()
    for first in range(0, LEAVES, 2):
        at = slice(first * RANK, first * RANK + 128)
        cr, ci, fr, fi = cback[0, :, at], cback[1, :, at], fback[0, :, at], fback[1, :, at]
        for s in (first, first + 1):
            if s == first:
                re, im = jnp.where(low, cr, fr), jnp.where(low, ci, fi)
                two = (co_v, fo_v)
            else:
                re, im = jnp.where(low, fr, cr), jnp.where(low, fi, ci)
                two = (fo_v, co_v)
            left = jnp.concatenate(
                [jnp.concatenate([re, -im], axis=1), jnp.concatenate([im, re], axis=1)], axis=0
            ).astype(BF16)
            w = jnp.concatenate([two[0][0, s], two[1][0, s], two[0][1, s], two[1][1, s]], axis=0)
            out[:, :, s * LEAF : (s + 1) * LEAF] = dot(left, w).reshape(2, VECTORS, LEAF)

    sent(cs1, 0)
    sent(fs1.at[pl.ds(0, GROUPS - 1)], 1)
    sent(cs2.at[pl.ds(0, MEMBERS - 1)], 2)
    sent(fs2.at[pl.ds(0, MEMBERS - 1)], 3)


def local(*args):
    hbm = pl.BlockSpec(memory_space=pltpu.HBM)
    shapes = [a.shape for a in args]
    vmem = pltpu.VMEM
    return pl.pallas_call(
        kernel,
        out_shape=jax.ShapeDtypeStruct(shapes[0], F32),
        in_specs=[hbm] * len(args),
        out_specs=pl.BlockSpec(memory_space=pltpu.VMEM),
        scratch_shapes=[
            vmem(shapes[0], F32),
            *[vmem(s, BF16) for s in shapes[1:9]],
            pltpu.SMEM(shapes[9], jnp.int32),
            vmem((256, 256), BF16),
            vmem((256, 512), BF16),
            vmem((256, 512), BF16),
            vmem((64, 1024), BF16),
            vmem((64, 1024), BF16),
            vmem((2, 32, 1024), F32),
            vmem((2, 32, 1024), F32),
            *[
                vmem(s, BF16)
                for s in [
                    (GROUPS, ROWS, 128), (GROUPS, ROWS, 128), (MEMBERS, 2 * GROUPS, 128), (MEMBERS, 2 * GROUPS, 128),
                ]
                * 2
            ],
            pltpu.SemaphoreType.DMA((1 + 3 * CHUNKS + 6,)),
            pltpu.SemaphoreType.DMA((4,)),
            pltpu.SemaphoreType.DMA((4,)),
        ],
        compiler_params=pltpu.CompilerParams(
            collective_id=0, has_side_effects=True, vmem_limit_bytes=40 * 1024 * 1024
        ),
        cost_estimate=pl.CostEstimate(flops=672 * 10**6, bytes_accessed=12 * 2**20, transcendentals=0),
    )(*[pltpu.with_memory_space_constraint(a, pltpu.HBM) for a in args])


def solution(mesh):
    return jax.shard_map(
        local,
        mesh=mesh,
        in_specs=(
            P(None, None, ("half", "bf")),
            P(None, ("half", "bf"), None, None),
            P(None, ("half", "bf"), None, None),
            P(None, ("half", "bf"), None, None),
            P(None, ("half", "bf"), None, None),
            P(None, ("half", "bf"), None, None),
            P(None, ("half", "bf"), None, None, None),
            P(None, ("half", "bf"), None, None, None),
            P(None, ("half", "bf"), None, None),
            P(None, ("half", "bf")),
        ),
        out_specs=P(None, None, ("half", "bf")),
        check_vma=False,
    )
```

```python
import functools

import jax
import jax.numpy as jnp
from jax import lax
from jax.experimental import pallas as pl
from jax.experimental.pallas import tpu as pltpu
from jax.sharding import PartitionSpec as P

F32 = jnp.float32
BF16 = jnp.bfloat16
MESH = pl.DeviceIdType.MESH
CORES = 2
CHIPS = 64
RING = 4
LEAVES = 16
RANK = 64
LEAF = 256
VECTORS = 32
CHUNKS = 2


def dot(left, right):
    return lax.dot_general(left, right, (((1,), (0,)), ((), ())), preferred_element_type=F32)


def dot_t(left, right):
    return lax.dot_general(left, right, (((1,), (1,)), ((), ())), preferred_element_type=F32)


def iota(shape, axis):
    return lax.broadcasted_iota(jnp.int32, shape, axis)


def farthest_first(apart):
    ways = [(0, 1.5, 2, 1.5), (4, 2.5, 2, 2.5)][apart]
    ring = (0, 1, 2, 1)
    steps = [(z, y, x) for z in range(RING) for y in range(RING) for x in range(RING)]
    return sorted(steps, key=lambda s: -(ways[s[0]] + ring[s[1]] + ring[s[2]]))


def complex_rows(by_real, by_imag):
    n = VECTORS
    return by_real[:n] - by_imag[n:], by_real[n:] + by_imag[:n]


def kernel(
    sources, coarse_in, coarse_mix_in, coarse_mix_out, coarse_out,
    fine_in, fine_mix_in, fine_mix_out, fine_out, ranks,
    out,
    x_v, ci_v, cmi_v, cmo_v, co_v, fi_v, fmi_v, fmo_v, fo_v, ranks_s,
    square, wide, ccoef, fcoef, cback, fback,
    c_put, c_got, c_core, f_put, f_got, f_core,
    in_sem, send_sem, recv_sem,
):
    half = lax.axis_index("half")
    block = lax.axis_index("bf")
    core = block % CORES
    chip = block // CORES
    at_z, at_y, at_x = chip // (RING * RING), chip // RING % RING, chip % RING
    zs = [(at_z + k) % RING * (RING * RING) for k in range(RING)]
    ys = [(at_y + k) % RING * RING for k in range(RING)]
    xs = [(at_x + k) % RING for k in range(RING)]

    def chips(apart):
        return [zs[z] + ys[y] + xs[x] for z, y, x in farthest_first(apart) if apart or z + y + x]

    barrier = pltpu.get_barrier_semaphore()

    def greet(h, b):
        pl.semaphore_signal(barrier, inc=1, device_id=(h, b), device_id_type=MESH)

    per = LEAVES // CHUNKS
    loads = {}

    def load(name, source, target):
        copy = pltpu.make_async_copy(source, target, in_sem.at[len(loads)])
        copy.start()
        loads[name] = copy

    load("ranks", ranks, ranks_s)
    for c in range(CHUNKS):
        span = pl.ds(c * per, per)
        cols = pl.ds(c * per * LEAF, per * LEAF)
        load(("x", c), sources.at[:, :, cols], x_v.at[:, :, cols])
        load(("ci", c), coarse_in.at[:, span], ci_v.at[:, span])
        load(("fi", c), fine_in.at[:, span], fi_v.at[:, span])
    load("cmi", coarse_mix_in, cmi_v)
    load("fmi", fine_mix_in, fmi_v)
    for there in chips(1):
        greet(1 - half, there * CORES + core)
    for there in chips(0):
        greet(half, there * CORES + core)
    greet(half, chip * CORES + 1 - core)
    load("fmo", fine_mix_out, fmo_v)
    load("cmo", coarse_mix_out, cmo_v)
    load("co", coarse_out, co_v)
    load("fo", fine_out, fo_v)

    def taken(row):
        return row % 128 // 2 * 4 + (core + row // 128) % 2 * 2 + row % 2

    square[...] = (taken(iota((256, 256), 0)) == iota((256, 256), 1)).astype(F32).astype(BF16)
    wide[...] = (taken(iota((256, 512), 0)) == iota((256, 512), 1) // 2).astype(F32).astype(BF16)

    lane = iota((1, 128), 1)
    low = lane < RANK

    def keep(first, second):
        return lane < jnp.where(low, first, second + RANK)

    loads["ranks"].wait()
    for c in range(CHUNKS):
        for name in ("x", "ci", "fi"):
            loads[name, c].wait()
        for first in range(c * per, (c + 1) * per, 2):
            got = []
            for s in (first, first + 1):
                x = x_v[:, :, s * LEAF : (s + 1) * LEAF].astype(BF16).reshape(2 * VECTORS, LEAF)
                two = (ci_v, fi_v) if s == first else (fi_v, ci_v)
                w = jnp.concatenate([two[0][0, s], two[1][0, s], two[0][1, s], two[1][1, s]], axis=0)
                y = dot_t(x, w)
                re, im = complex_rows(y[:, :128], y[:, 128:])
                which = (0, 2) if s == first else (2, 0)
                kept = keep(ranks_s[which[0], s], ranks_s[which[1], s])
                both = jnp.concatenate([re, im], axis=0)
                got.append(jnp.where(kept, both, 0.0))
            at = pl.ds(first * RANK, 2 * RANK)
            ccoef[:, at] = jnp.where(low, got[0], got[1]).astype(BF16)
            fcoef[:, at] = jnp.where(low, got[1], got[0]).astype(BF16)

    def remote(source, target, which, h, b):
        pltpu.make_async_remote_copy(
            src_ref=source, dst_ref=target, send_sem=send_sem.at[which], recv_sem=recv_sem.at[which],
            device_id=(h, b), device_id_type=MESH,
        ).start()

    def arrived(buffer, which):
        pltpu.make_async_copy(buffer, buffer, recv_sem.at[which]).wait()

    def sent(buffer, which):
        pltpu.make_async_copy(buffer, buffer, send_sem.at[which]).wait()

    loads["cmi"].wait()
    re, im = complex_rows(dot(ccoef[...], cmi_v[0, 0]), dot(ccoef[...], cmi_v[1, 0]))
    send = jnp.concatenate([re, im], axis=0)
    even = iota((1, 512), 1) % 2 == 0
    send = jnp.concatenate([jnp.where(even, send, 0.0), jnp.where(even, 0.0, send)], axis=0).astype(BF16)
    c_put[...] = dot_t(wide[...], send).astype(BF16).reshape(c_put.shape)

    def send_coarse():
        for there in chips(1):
            remote(c_put.at[:, there], c_got.at[:, chip], 0, 1 - half, there * CORES + core)

    @pl.when(half == 1)
    def _():
        pl.semaphore_wait(barrier, 2 * CHIPS)
        send_coarse()

    loads["fmi"].wait()
    fine = []
    for i in range(2):
        left = fcoef[:, i * 512 : (i + 1) * 512]
        parts = []
        for part in range(2):
            order = [leaf ^ 1 for leaf in range(LEAVES // 2)]
            w = jnp.concatenate(
                [fmi_v[part, 0, i, leaf * RANK : (leaf + 1) * RANK, :] for leaf in order], axis=0
            )
            parts.append(dot(left, w))
        fine.extend(complex_rows(*parts))
    send = jnp.concatenate(fine, axis=0)
    f_put[...] = dot_t(square[...], send.astype(BF16)).astype(BF16).reshape(f_put.shape)
    @pl.when(half == 0)
    def _():
        pl.semaphore_wait(barrier, 2 * CHIPS)

    for there in chips(0):
        remote(f_put.at[:, there], f_got.at[:, chip], 1, half, there * CORES + core)
    pltpu.make_async_copy(f_put.at[:, chip], f_got.at[:, chip], recv_sem.at[1]).start()

    @pl.when(half == 0)
    def _():
        send_coarse()

    def rows_of(got, landing, which):
        arrived(landing, which)
        return jnp.concatenate([got[0].reshape(128, 128), landing[...].reshape(128, 128)], axis=0)

    arrived(f_got, 1)
    remote(f_got.at[1], f_core, 3, half, chip * CORES + 1 - core)
    got = dot(rows_of(f_got, f_core, 3).T, square[...]).astype(BF16)
    loads["fmo"].wait()
    for i in range(2):
        left = got[i * 64 : i * 64 + 64]
        for at in range(0, 512, 256):
            re, im = complex_rows(
                dot(left, fmo_v[0, 0, i, :, at : at + 256]), dot(left, fmo_v[1, 0, i, :, at : at + 256])
            )
            for n in range(2):
                place = (1 - i) * 512 + at + 128 * n
                leaf = place // RANK
                kept = keep(ranks_s[3, leaf], ranks_s[3, leaf + 1])
                cols = slice(128 * n, 128 * n + 128)
                fback[0, :, place : place + 128] = pltpu.roll(jnp.where(kept, re[:, cols], 0.0), RANK, 1)
                fback[1, :, place : place + 128] = pltpu.roll(jnp.where(kept, im[:, cols], 0.0), RANK, 1)

    arrived(c_got, 0)
    remote(c_got.at[1], c_core, 2, half, chip * CORES + 1 - core)
    got = dot(rows_of(c_got, c_core, 2).T, wide[...])
    left = jnp.where(even, got[:64], got[64:]).astype(BF16)
    loads["cmo"].wait()
    for at in range(0, 1024, 256):
        re, im = complex_rows(dot(left, cmo_v[0, 0, :, at : at + 256]), dot(left, cmo_v[1, 0, :, at : at + 256]))
        for n in range(2):
            leaf = at // RANK + 2 * n
            kept = keep(ranks_s[1, leaf], ranks_s[1, leaf + 1])
            cols = slice(128 * n, 128 * n + 128)
            cback[0, :, at + 128 * n : at + 128 * n + 128] = jnp.where(kept, re[:, cols], 0.0)
            cback[1, :, at + 128 * n : at + 128 * n + 128] = jnp.where(kept, im[:, cols], 0.0)

    loads["co"].wait()
    loads["fo"].wait()
    for first in range(0, LEAVES, 2):
        at = slice(first * RANK, first * RANK + 128)
        cr, ci, fr, fi = cback[0, :, at], cback[1, :, at], fback[0, :, at], fback[1, :, at]
        for s in (first, first + 1):
            if s == first:
                re, im = jnp.where(low, cr, fr), jnp.where(low, ci, fi)
                two = (co_v, fo_v)
            else:
                re, im = jnp.where(low, fr, cr), jnp.where(low, fi, ci)
                two = (fo_v, co_v)
            left = jnp.concatenate(
                [jnp.concatenate([re, -im], axis=1), jnp.concatenate([im, re], axis=1)], axis=0
            ).astype(BF16)
            w = jnp.concatenate([two[0][0, s], two[1][0, s], two[0][1, s], two[1][1, s]], axis=0)
            out[:, :, s * LEAF : (s + 1) * LEAF] = dot(left, w).reshape(2, VECTORS, LEAF)

    sent(c_put, 0)
    sent(f_put.at[:, pl.ds(0, CHIPS - 1)], 1)
    sent(c_core, 2)
    sent(f_core, 3)


def local(*args):
    hbm = pl.BlockSpec(memory_space=pltpu.HBM)
    shapes = [a.shape for a in args]
    vmem = pltpu.VMEM
    return pl.pallas_call(
        kernel,
        out_shape=jax.ShapeDtypeStruct(shapes[0], F32),
        in_specs=[hbm] * len(args),
        out_specs=pl.BlockSpec(memory_space=pltpu.VMEM),
        scratch_shapes=[
            vmem(shapes[0], F32),
            *[vmem(s, BF16) for s in shapes[1:9]],
            pltpu.SMEM(shapes[9], jnp.int32),
            vmem((256, 256), BF16),
            vmem((256, 512), BF16),
            vmem((64, 1024), BF16),
            vmem((64, 1024), BF16),
            vmem((2, 32, 1024), F32),
            vmem((2, 32, 1024), F32),
            *[vmem(s, BF16) for s in [(CORES, CHIPS, 2, 128), (CORES, CHIPS, 2, 128), (CHIPS, 2, 128)] * 2],
            pltpu.SemaphoreType.DMA((1 + 3 * CHUNKS + 6,)),
            pltpu.SemaphoreType.DMA((4,)),
            pltpu.SemaphoreType.DMA((4,)),
        ],
        compiler_params=pltpu.CompilerParams(
            collective_id=0, has_side_effects=True, vmem_limit_bytes=40 * 1024 * 1024
        ),
        cost_estimate=pl.CostEstimate(flops=672 * 10**6, bytes_accessed=12 * 2**20, transcendentals=0),
    )(*[pltpu.with_memory_space_constraint(a, pltpu.HBM) for a in args])


def solution(mesh):
    return jax.shard_map(
        local,
        mesh=mesh,
        in_specs=(
            P(None, None, ("half", "bf")),
            P(None, ("half", "bf"), None, None),
            P(None, ("half", "bf"), None, None),
            P(None, ("half", "bf"), None, None),
            P(None, ("half", "bf"), None, None),
            P(None, ("half", "bf"), None, None),
            P(None, ("half", "bf"), None, None, None),
            P(None, ("half", "bf"), None, None, None),
            P(None, ("half", "bf"), None, None),
            P(None, ("half", "bf")),
        ),
        out_specs=P(None, None, ("half", "bf")),
        check_vma=False,
    )
```

```python
import functools

import jax
import jax.numpy as jnp
from jax import lax
from jax.experimental import pallas as pl
from jax.experimental.pallas import tpu as pltpu
from jax.sharding import PartitionSpec as P

F32 = jnp.float32
BF16 = jnp.bfloat16
MESH = pl.DeviceIdType.MESH
CORES = 2
CHIPS = 64
RING = 4
LEAVES = 16
RANK = 64
LEAF = 256
VECTORS = 32
CHUNKS = 2
MIX_CHUNKS = 4


def dot(left, right):
    return lax.dot_general(left, right, (((1,), (0,)), ((), ())), preferred_element_type=F32)


def dot_t(left, right):
    return lax.dot_general(left, right, (((1,), (1,)), ((), ())), preferred_element_type=F32)


def iota(shape, axis):
    return lax.broadcasted_iota(jnp.int32, shape, axis)


def farthest_first(apart):
    ways = [(0, 1.5, 2, 1.5), (4, 2.5, 2, 2.5)][apart]
    ring = (0, 1, 2, 1)
    steps = [(z, y, x) for z in range(RING) for y in range(RING) for x in range(RING)]
    return sorted(steps, key=lambda s: -(ways[s[0]] + ring[s[1]] + ring[s[2]]))


def complex_rows(by_real, by_imag):
    n = VECTORS
    return by_real[:n] - by_imag[n:], by_real[n:] + by_imag[:n]


def kernel(
    sources, coarse_in, coarse_mix_in, coarse_mix_out, coarse_out,
    fine_in, fine_mix_in, fine_mix_out, fine_out, ranks,
    out,
    x_v, ci_v, cmi_v, cmo_v, co_v, fi_v, fmi_v, fmo_v, fo_v, ranks_s,
    square, wide, ccoef, fcoef, fback,
    c_put, c_got, c_core, f_put, f_got, f_core,
    in_sem, send_sem, recv_sem, coarse_ok, fine_ok,
):
    half = lax.axis_index("half")
    block = lax.axis_index("bf")
    core = block % CORES
    chip = block // CORES
    at_z, at_y, at_x = chip // (RING * RING), chip // RING % RING, chip % RING
    zs = [(at_z + k) % RING * (RING * RING) for k in range(RING)]
    ys = [(at_y + k) % RING * RING for k in range(RING)]
    xs = [(at_x + k) % RING for k in range(RING)]

    def chips(apart):
        return [zs[z] + ys[y] + xs[x] for z, y, x in farthest_first(apart) if apart or z + y + x]

    barrier = pltpu.get_barrier_semaphore()

    def greet(h, b):
        pl.semaphore_signal(barrier, inc=1, device_id=(h, b), device_id_type=MESH)

    per = LEAVES // CHUNKS
    deep = LEAVES * RANK // MIX_CHUNKS
    loads = {}

    def load(name, source, target):
        copy = pltpu.make_async_copy(source, target, in_sem.at[len(loads)])
        copy.start()
        loads[name] = copy

    load("ranks", ranks, ranks_s)
    for c in range(CHUNKS):
        span = pl.ds(c * per, per)
        cols = pl.ds(c * per * LEAF, per * LEAF)
        load(("x", c), sources.at[:, :, cols], x_v.at[:, :, cols])
        load(("ci", c), coarse_in.at[:, span], ci_v.at[:, span])
    for c in range(MIX_CHUNKS):
        span = pl.ds(c * deep, deep)
        load(("cmi", c), coarse_mix_in.at[:, :, span], cmi_v.at[:, :, span])
    load("fi", fine_in, fi_v)
    load("fmi", fine_mix_in, fmi_v)
    greet(half, chip * CORES + 1 - core)
    for there in chips(1):
        greet(1 - half, there * CORES + 1)
    for there in chips(0):
        greet(half, there * CORES)

    def tell(semaphore):
        to = (half, chip * CORES + 1 - core)
        pl.semaphore_signal(semaphore, inc=1, device_id=to, device_id_type=MESH)

    def hear_other_half():
        pl.semaphore_wait(barrier, CORES * CHIPS + 1)
        tell(coarse_ok)

    load("fmo", fine_mix_out, fmo_v)
    load("cmo", coarse_mix_out, cmo_v)
    load("co", coarse_out, co_v)
    load("fo", fine_out, fo_v)

    def taken(row):
        return row % 128 // 2 * 4 + (core + row // 128) % 2 * 2 + row % 2

    square[...] = (taken(iota((256, 256), 0)) == iota((256, 256), 1)).astype(F32).astype(BF16)
    wide[...] = (taken(iota((256, 512), 0)) == iota((256, 512), 1) // 2).astype(F32).astype(BF16)

    lane = iota((1, 128), 1)
    low = lane < RANK

    def keep(first, second):
        return lane < jnp.where(low, first, second + RANK)

    def swapped(two):
        return pltpu.roll(two, RANK, 1)

    def column_pair(factor, which, first):
        mixed = []
        for s in (first, first + 1):
            x = x_v[:, :, s * LEAF : (s + 1) * LEAF].astype(BF16).reshape(2 * VECTORS, LEAF)
            order = (0, 1) if s == first else (1, 0)
            y = dot_t(x, jnp.concatenate([factor[order[0], s], factor[order[1], s]], axis=0))
            mine, other = y[:VECTORS], swapped(y[VECTORS:])
            mixed.append(mine + jnp.where(low == (s == first), -other, other))
        both = [jnp.where(low, mixed[0], mixed[1]), swapped(jnp.where(low, mixed[1], mixed[0]))]
        kept = keep(ranks_s[which, first], ranks_s[which, first + 1])
        return jnp.where(kept, jnp.concatenate(both, axis=0), 0.0).astype(BF16)

    loads["ranks"].wait()
    for c in range(CHUNKS):
        loads["x", c].wait()
        loads["ci", c].wait()
        for first in range(c * per, (c + 1) * per, 2):
            ccoef[:, first * RANK : (first + 2) * RANK] = column_pair(ci_v, 0, first)

    def remote(source, target, which, h, b, out=None):
        pltpu.make_async_remote_copy(
            src_ref=source, dst_ref=target, send_sem=send_sem.at[which if out is None else out], recv_sem=recv_sem.at[which],
            device_id=(h, b), device_id_type=MESH,
        ).start()

    def arrived(buffer, which):
        pltpu.make_async_copy(buffer, buffer, recv_sem.at[which]).wait()

    def sent(buffer, which):
        pltpu.make_async_copy(buffer, buffer, send_sem.at[which]).wait()

    @pl.when((half == 1) & (core == 1))
    def _():
        hear_other_half()

    sums = [0.0, 0.0]
    for c in range(MIX_CHUNKS):
        loads["cmi", c].wait()
        span = slice(c * deep, (c + 1) * deep)
        sums = [sums[part] + dot(ccoef[:, span], cmi_v[part, 0, span]) for part in range(2)]
    re, im = complex_rows(*sums)
    send = jnp.concatenate([re, im], axis=0)
    even = iota((1, 512), 1) % 2 == 0
    send = jnp.concatenate([jnp.where(even, send, 0.0), jnp.where(even, 0.0, send)], axis=0).astype(BF16)
    c_put[...] = dot_t(wide[...], send).astype(BF16).reshape(c_put.shape)

    def send_coarse(direct):
        for there in chips(1):
            if direct:
                for k, target in enumerate((c_got.at[0, chip], c_core.at[chip])):
                    to = there * CORES + (core + k) % CORES
                    remote(c_put.at[k, there], target, 2 * k, 0, to)
            else:
                remote(c_put.at[:, there], c_got.at[:, chip], 0, 1, there * CORES + core)

    @pl.when((half == 1) & (core == 0))
    def _():
        pl.semaphore_wait(coarse_ok, 1)

    @pl.when(half == 1)
    def _():
        send_coarse(True)

    loads["fi"].wait()
    for first in range(0, LEAVES, 2):
        fcoef[:, first * RANK : (first + 2) * RANK] = column_pair(fi_v, 2, first)
    loads["fmi"].wait()
    fine = []
    for i in range(2):
        left = fcoef[:, i * 512 : (i + 1) * 512]
        fine.extend(complex_rows(dot(left, fmi_v[0, 0, i]), dot(left, fmi_v[1, 0, i])))
    send = jnp.concatenate(fine, axis=0)
    f_put[...] = dot_t(square[...], send.astype(BF16)).astype(BF16).reshape(f_put.shape)
    @pl.when(core == 0)
    def _():
        pl.semaphore_wait(barrier, CORES * (CHIPS - 1) + 1)
        tell(fine_ok)

    @pl.when(core == 1)
    def _():
        pl.semaphore_wait(fine_ok, 1)

    for there in chips(0):
        remote(f_put.at[:, there], f_got.at[:, chip], 1, half, there * CORES + core)
    pltpu.make_async_copy(f_put.at[:, chip], f_got.at[:, chip], recv_sem.at[1]).start()

    @pl.when((half == 0) & (core == 1))
    def _():
        hear_other_half()

    @pl.when((half == 0) & (core == 0))
    def _():
        pl.semaphore_wait(coarse_ok, 1)

    @pl.when(half == 0)
    def _():
        send_coarse(False)

    def rows_of(got, landing, which):
        arrived(landing, which)
        return jnp.concatenate([got[0].reshape(128, 128), landing[...].reshape(128, 128)], axis=0)

    arrived(f_got, 1)
    remote(f_got.at[1], f_core, 3, half, chip * CORES + 1 - core)
    got = dot(rows_of(f_got, f_core, 3).T, square[...]).astype(BF16)
    loads["fmo"].wait()
    for i in range(2):
        left = got[i * 64 : i * 64 + 64]
        for at in range(0, 512, 256):
            re, im = complex_rows(
                dot(left, fmo_v[0, 0, i, :, at : at + 256]), dot(left, fmo_v[1, 0, i, :, at : at + 256])
            )
            for n in range(2):
                place = (1 - i) * 512 + at + 128 * n
                leaf = place // RANK
                kept = keep(ranks_s[3, leaf], ranks_s[3, leaf + 1])
                cols = slice(128 * n, 128 * n + 128)
                fback[0, :, place : place + 128] = pltpu.roll(jnp.where(kept, re[:, cols], 0.0), RANK, 1)
                fback[1, :, place : place + 128] = pltpu.roll(jnp.where(kept, im[:, cols], 0.0), RANK, 1)

    @pl.when(half == 0)
    def _():
        arrived(c_got.at[0], 0)

    @pl.when(half == 1)
    def _():
        arrived(c_got, 0)
        remote(c_got.at[1], c_core, 2, 1, chip * CORES + 1 - core, 4)

    got = dot(rows_of(c_got, c_core, 2).T, wide[...])
    left = jnp.where(even, got[:64], got[64:]).astype(BF16)
    loads["cmo"].wait()
    loads["co"].wait()
    loads["fo"].wait()
    for at in range(0, 1024, 256):
        pair = complex_rows(dot(left, cmo_v[0, 0, :, at : at + 256]), dot(left, cmo_v[1, 0, :, at : at + 256]))
        for n in range(2):
            first = at // RANK + 2 * n
            kept = keep(ranks_s[1, first], ranks_s[1, first + 1])
            cr, ci = [jnp.where(kept, part[:, 128 * n : 128 * n + 128], 0.0) for part in pair]
            cols = slice(first * RANK, first * RANK + 128)
            fr, fi = fback[0, :, cols], fback[1, :, cols]
            for s in (first, first + 1):
                if s == first:
                    re, im = jnp.where(low, cr, fr), jnp.where(low, ci, fi)
                    two = (co_v, fo_v)
                else:
                    re, im = jnp.where(low, fr, cr), jnp.where(low, fi, ci)
                    two = (fo_v, co_v)
                rows = [jnp.concatenate([re, -im], axis=1), jnp.concatenate([im, re], axis=1)]
                w = jnp.concatenate([two[0][0, s], two[1][0, s], two[0][1, s], two[1][1, s]], axis=0)
                y = dot(jnp.concatenate(rows, axis=0).astype(BF16), w)
                out[:, :, s * LEAF : (s + 1) * LEAF] = y.reshape(2, VECTORS, LEAF)

    @pl.when(half == 0)
    def _():
        sent(c_put, 0)

    @pl.when(half == 1)
    def _():
        sent(c_put.at[0], 0)
        sent(c_put.at[1], 2)
        sent(c_core, 4)

    sent(f_put.at[:, pl.ds(0, CHIPS - 1)], 1)
    sent(f_core, 3)


def local(*args):
    hbm = pl.BlockSpec(memory_space=pltpu.HBM)
    shapes = [a.shape for a in args]
    vmem = pltpu.VMEM
    return pl.pallas_call(
        kernel,
        out_shape=jax.ShapeDtypeStruct(shapes[0], F32),
        in_specs=[hbm] * len(args),
        out_specs=pl.BlockSpec(memory_space=pltpu.VMEM),
        scratch_shapes=[
            vmem(shapes[0], F32),
            *[vmem(s, BF16) for s in shapes[1:9]],
            pltpu.SMEM(shapes[9], jnp.int32),
            vmem((256, 256), BF16),
            vmem((256, 512), BF16),
            vmem((64, 1024), BF16),
            vmem((64, 1024), BF16),
            vmem((2, 32, 1024), F32),
            *[vmem(s, BF16) for s in [(CORES, CHIPS, 2, 128), (CORES, CHIPS, 2, 128), (CHIPS, 2, 128)] * 2],
            pltpu.SemaphoreType.DMA((1 + 2 * CHUNKS + MIX_CHUNKS + 6,)),
            pltpu.SemaphoreType.DMA((5,)),
            pltpu.SemaphoreType.DMA((4,)),
            pltpu.SemaphoreType.REGULAR,
            pltpu.SemaphoreType.REGULAR,
        ],
        compiler_params=pltpu.CompilerParams(
            collective_id=0, has_side_effects=True, vmem_limit_bytes=40 * 1024 * 1024
        ),
        cost_estimate=pl.CostEstimate(flops=672 * 10**6, bytes_accessed=12 * 2**20, transcendentals=0),
    )(*[pltpu.with_memory_space_constraint(a, pltpu.HBM) for a in args])


def solution(mesh):
    return jax.shard_map(
        local,
        mesh=mesh,
        in_specs=(
            P(None, None, ("half", "bf")),
            P(None, ("half", "bf"), None, None),
            P(None, ("half", "bf"), None, None),
            P(None, ("half", "bf"), None, None),
            P(None, ("half", "bf"), None, None),
            P(None, ("half", "bf"), None, None),
            P(None, ("half", "bf"), None, None, None),
            P(None, ("half", "bf"), None, None, None),
            P(None, ("half", "bf"), None, None),
            P(None, ("half", "bf")),
        ),
        out_specs=P(None, None, ("half", "bf")),
        check_vma=False,
    )
```

```python
import functools

import jax
import jax.numpy as jnp
from jax import lax
from jax.experimental import pallas as pl
from jax.experimental.pallas import tpu as pltpu
from jax.sharding import PartitionSpec as P

F32 = jnp.float32
BF16 = jnp.bfloat16
MESH = pl.DeviceIdType.MESH
CORES = 2
CHIPS = 64
PART = 32
RING = 4
LEAVES = 16
RANK = 64
LEAF = 256
VECTORS = 32
CHUNKS = 2
MIX_CHUNKS = 4


def dot(left, right):
    return lax.dot_general(left, right, (((1,), (0,)), ((), ())), preferred_element_type=F32)


def dot_t(left, right):
    return lax.dot_general(left, right, (((1,), (1,)), ((), ())), preferred_element_type=F32)


def iota(shape, axis):
    return lax.broadcasted_iota(jnp.int32, shape, axis)


def farthest_first(apart):
    ways = [(0, 1.5, 2, 1.5), (4, 2.5, 2, 2.5)][apart]
    ring = (0, 1, 2, 1)
    steps = [(z, y, x) for z in range(RING) for y in range(RING) for x in range(RING)]
    return sorted(steps, key=lambda s: -(ways[s[0]] + ring[s[1]] + ring[s[2]]))


def complex_rows(by_real, by_imag):
    n = VECTORS
    return by_real[:n] - by_imag[n:], by_real[n:] + by_imag[:n]


def kernel(
    sources, coarse_in, coarse_mix_in, coarse_mix_out, coarse_out,
    fine_in, fine_mix_in, fine_mix_out, fine_out, ranks,
    out,
    x_v, ci_v, cmi_v, cmo_v, co_v, fi_v, fmi_v, fmo_v, fo_v, ranks_s,
    square, wide, ccoef, fcoef, fback,
    c_put, c_got, c_core, f_put, f_got, f_core,
    in_sem, send_sem, recv_sem, coarse_ok, fine_ok,
):
    half = lax.axis_index("half")
    block = lax.axis_index("bf")
    core = block % CORES
    chip = block // CORES
    at_z, at_y, at_x = chip // (RING * RING), chip // RING % RING, chip % RING
    zs = [(at_z + k) % RING * (RING * RING) for k in range(RING)]
    ys = [(at_y + k) % RING * RING for k in range(RING)]
    xs = [(at_x + k) % RING for k in range(RING)]

    def chips(apart):
        return [zs[z] + ys[y] + xs[x] for z, y, x in farthest_first(apart) if apart or z + y + x]

    barrier = pltpu.get_barrier_semaphore()

    def greet(h, b):
        pl.semaphore_signal(barrier, inc=1, device_id=(h, b), device_id_type=MESH)

    per = LEAVES // CHUNKS
    deep = LEAVES * RANK // MIX_CHUNKS
    loads = {}

    def load(name, source, target):
        copy = pltpu.make_async_copy(source, target, in_sem.at[len(loads)])
        copy.start()
        loads[name] = copy

    load("ranks", ranks, ranks_s)
    for c in range(CHUNKS):
        span = pl.ds(c * per, per)
        cols = pl.ds(c * per * LEAF, per * LEAF)
        load(("x", c), sources.at[:, :, cols], x_v.at[:, :, cols])
        load(("ci", c), coarse_in.at[:, span], ci_v.at[:, span])
    for c in range(MIX_CHUNKS):
        span = pl.ds(c * deep, deep)
        load(("cmi", c), coarse_mix_in.at[:, :, span], cmi_v.at[:, :, span])
    load("fi", fine_in, fi_v)
    load("fmi", fine_mix_in, fmi_v)
    greet(half, chip * CORES + 1 - core)
    for there in chips(1):
        greet(1 - half, there * CORES + 1)
    for there in chips(0):
        greet(half, there * CORES)

    def tell(semaphore):
        to = (half, chip * CORES + 1 - core)
        pl.semaphore_signal(semaphore, inc=1, device_id=to, device_id_type=MESH)

    def hear_other_half():
        pl.semaphore_wait(barrier, CORES * CHIPS + 1)
        tell(coarse_ok)

    load("fmo", fine_mix_out, fmo_v)
    load("cmo", coarse_mix_out, cmo_v)
    load("co", coarse_out, co_v)
    load("fo", fine_out, fo_v)

    def taken(row):
        return row % (2 * PART) // 2 * 4 + (core + row // (2 * PART)) % 2 * 2 + row % 2

    square[...] = (taken(iota(square.shape, 0)) == iota(square.shape, 1)).astype(F32).astype(BF16)
    wide[...] = (taken(iota(wide.shape, 0)) == iota(wide.shape, 1) // 2).astype(F32).astype(BF16)

    lane = iota((1, 128), 1)
    low = lane < RANK

    def keep(first, second):
        return lane < jnp.where(low, first, second + RANK)

    def swapped(two):
        return pltpu.roll(two, RANK, 1)

    def column_pair(factor, which, first):
        mixed = []
        for s in (first, first + 1):
            x = x_v[:, :, s * LEAF : (s + 1) * LEAF].astype(BF16).reshape(2 * VECTORS, LEAF)
            order = (0, 1) if s == first else (1, 0)
            y = dot_t(x, jnp.concatenate([factor[order[0], s], factor[order[1], s]], axis=0))
            mine, other = y[:VECTORS], swapped(y[VECTORS:])
            mixed.append(mine + jnp.where(low == (s == first), -other, other))
        both = [jnp.where(low, mixed[0], mixed[1]), swapped(jnp.where(low, mixed[1], mixed[0]))]
        kept = keep(ranks_s[which, first], ranks_s[which, first + 1])
        return jnp.where(kept, jnp.concatenate(both, axis=0), 0.0).astype(BF16)

    loads["ranks"].wait()
    for c in range(CHUNKS):
        loads["x", c].wait()
        loads["ci", c].wait()
        for first in range(c * per, (c + 1) * per, 2):
            ccoef[:, first * RANK : (first + 2) * RANK] = column_pair(ci_v, 0, first)

    def remote(source, target, which, h, b, out=None):
        pltpu.make_async_remote_copy(
            src_ref=source, dst_ref=target, send_sem=send_sem.at[which if out is None else out], recv_sem=recv_sem.at[which],
            device_id=(h, b), device_id_type=MESH,
        ).start()

    def arrived(buffer, which):
        pltpu.make_async_copy(buffer, buffer, recv_sem.at[which]).wait()

    def sent(buffer, which):
        pltpu.make_async_copy(buffer, buffer, send_sem.at[which]).wait()

    sums = [0.0, 0.0]
    for c in range(MIX_CHUNKS):
        loads["cmi", c].wait()
        span = slice(c * deep, (c + 1) * deep)
        sums = [sums[part] + dot(ccoef[:, span], cmi_v[part, 0, span]) for part in range(2)]
    re, im = complex_rows(*sums)
    send = jnp.concatenate([re, im], axis=0)
    even = iota((1, 8 * PART), 1) % 2 == 0

    def put(target, matrix, values):
        for at in range(0, CHIPS, PART):
            step = matrix.shape[1] // PART
            part = values[:, at * step : (at + PART) * step]
            if matrix is wide:
                part = jnp.concatenate([jnp.where(even, part, 0.0), jnp.where(even, 0.0, part)], axis=0)
            rows = dot_t(matrix[...], part.astype(BF16)).astype(BF16)
            for k in range(CORES):
                target[k, at : at + PART] = rows[k * 2 * PART : (k + 1) * 2 * PART].reshape(PART, 2, 128)

    put(c_put, wide, send)

    def send_coarse(direct):
        for there in chips(1):
            if direct:
                for k, target in enumerate((c_got.at[0, chip], c_core.at[chip])):
                    to = there * CORES + (core + k) % CORES
                    remote(c_put.at[k, there], target, 2 * k, 0, to)
            else:
                remote(c_put.at[:, there], c_got.at[:, chip], 0, 1, there * CORES + core)

    @pl.when((half == 1) & (core == 1))
    def _():
        hear_other_half()

    @pl.when((half == 1) & (core == 0))
    def _():
        pl.semaphore_wait(coarse_ok, 1)

    @pl.when(half == 1)
    def _():
        send_coarse(True)

    loads["fi"].wait()
    for first in range(0, LEAVES, 2):
        fcoef[:, first * RANK : (first + 2) * RANK] = column_pair(fi_v, 2, first)
    loads["fmi"].wait()
    fine = []
    for i in range(2):
        left = fcoef[:, i * 512 : (i + 1) * 512]
        fine.extend(complex_rows(dot(left, fmi_v[0, 0, i]), dot(left, fmi_v[1, 0, i])))
    send = jnp.concatenate(fine, axis=0)
    put(f_put, square, send)
    @pl.when(core == 0)
    def _():
        pl.semaphore_wait(barrier, CORES * (CHIPS - 1) + 1)
        tell(fine_ok)

    @pl.when(core == 1)
    def _():
        pl.semaphore_wait(fine_ok, 1)

    for there in chips(0):
        remote(f_put.at[:, there], f_got.at[:, chip], 1, half, there * CORES + core)
    pltpu.make_async_copy(f_put.at[:, chip], f_got.at[:, chip], recv_sem.at[1]).start()

    @pl.when((half == 0) & (core == 1))
    def _():
        hear_other_half()

    @pl.when((half == 0) & (core == 0))
    def _():
        pl.semaphore_wait(coarse_ok, 1)

    @pl.when(half == 0)
    def _():
        send_coarse(False)

    def columns(got, landing, matrix):
        parts = []
        for at in range(0, CHIPS, PART):
            two = [got[0, at : at + PART].reshape(2 * PART, 128), landing[at : at + PART].reshape(2 * PART, 128)]
            parts.append(dot(jnp.concatenate(two, axis=0).T, matrix[...]))
        if matrix is wide:
            parts = [jnp.where(even, part[:64], part[64:]) for part in parts]
        return jnp.concatenate(parts, axis=1).astype(BF16)

    arrived(f_got, 1)
    remote(f_got.at[1], f_core, 3, half, chip * CORES + 1 - core)
    arrived(f_core, 3)
    got = columns(f_got, f_core, square)
    loads["fmo"].wait()
    for i in range(2):
        left = got[i * 64 : i * 64 + 64]
        for at in range(0, 512, 256):
            re, im = complex_rows(
                dot(left, fmo_v[0, 0, i, :, at : at + 256]), dot(left, fmo_v[1, 0, i, :, at : at + 256])
            )
            for n in range(2):
                place = (1 - i) * 512 + at + 128 * n
                leaf = place // RANK
                kept = keep(ranks_s[3, leaf], ranks_s[3, leaf + 1])
                cols = slice(128 * n, 128 * n + 128)
                fback[0, :, place : place + 128] = pltpu.roll(jnp.where(kept, re[:, cols], 0.0), RANK, 1)
                fback[1, :, place : place + 128] = pltpu.roll(jnp.where(kept, im[:, cols], 0.0), RANK, 1)

    @pl.when(half == 0)
    def _():
        arrived(c_got.at[0], 0)

    @pl.when(half == 1)
    def _():
        arrived(c_got, 0)
        remote(c_got.at[1], c_core, 2, 1, chip * CORES + 1 - core, 4)

    arrived(c_core, 2)
    left = columns(c_got, c_core, wide)
    loads["cmo"].wait()
    loads["co"].wait()
    loads["fo"].wait()
    for at in range(0, 1024, 256):
        pair = complex_rows(dot(left, cmo_v[0, 0, :, at : at + 256]), dot(left, cmo_v[1, 0, :, at : at + 256]))
        for n in range(2):
            first = at // RANK + 2 * n
            kept = keep(ranks_s[1, first], ranks_s[1, first + 1])
            cr, ci = [jnp.where(kept, part[:, 128 * n : 128 * n + 128], 0.0) for part in pair]
            cols = slice(first * RANK, first * RANK + 128)
            fr, fi = fback[0, :, cols], fback[1, :, cols]
            for s in (first, first + 1):
                if s == first:
                    re, im = jnp.where(low, cr, fr), jnp.where(low, ci, fi)
                    two = (co_v, fo_v)
                else:
                    re, im = jnp.where(low, fr, cr), jnp.where(low, fi, ci)
                    two = (fo_v, co_v)
                rows = [jnp.concatenate([re, -im], axis=1), jnp.concatenate([im, re], axis=1)]
                w = jnp.concatenate([two[0][0, s], two[1][0, s], two[0][1, s], two[1][1, s]], axis=0)
                y = dot(jnp.concatenate(rows, axis=0).astype(BF16), w)
                out[:, :, s * LEAF : (s + 1) * LEAF] = y.reshape(2, VECTORS, LEAF)

    @pl.when(half == 0)
    def _():
        sent(c_put, 0)

    @pl.when(half == 1)
    def _():
        sent(c_put.at[0], 0)
        sent(c_put.at[1], 2)
        sent(c_core, 4)

    sent(f_put.at[:, pl.ds(0, CHIPS - 1)], 1)
    sent(f_core, 3)


def local(*args):
    hbm = pl.BlockSpec(memory_space=pltpu.HBM)
    shapes = [a.shape for a in args]
    vmem = pltpu.VMEM
    return pl.pallas_call(
        kernel,
        out_shape=jax.ShapeDtypeStruct(shapes[0], F32),
        in_specs=[hbm] * len(args),
        out_specs=pl.BlockSpec(memory_space=pltpu.VMEM),
        scratch_shapes=[
            vmem(shapes[0], F32),
            *[vmem(s, BF16) for s in shapes[1:9]],
            pltpu.SMEM(shapes[9], jnp.int32),
            vmem((4 * PART, 4 * PART), BF16),
            vmem((4 * PART, 8 * PART), BF16),
            vmem((64, 1024), BF16),
            vmem((64, 1024), BF16),
            vmem((2, 32, 1024), F32),
            *[vmem(s, BF16) for s in [(CORES, CHIPS, 2, 128), (CORES, CHIPS, 2, 128), (CHIPS, 2, 128)] * 2],
            pltpu.SemaphoreType.DMA((1 + 2 * CHUNKS + MIX_CHUNKS + 6,)),
            pltpu.SemaphoreType.DMA((5,)),
            pltpu.SemaphoreType.DMA((4,)),
            pltpu.SemaphoreType.REGULAR,
            pltpu.SemaphoreType.REGULAR,
        ],
        compiler_params=pltpu.CompilerParams(
            collective_id=0, has_side_effects=True, vmem_limit_bytes=40 * 1024 * 1024
        ),
        cost_estimate=pl.CostEstimate(flops=672 * 10**6, bytes_accessed=12 * 2**20, transcendentals=0),
    )(*[pltpu.with_memory_space_constraint(a, pltpu.HBM) for a in args])


def solution(mesh):
    return jax.shard_map(
        local,
        mesh=mesh,
        in_specs=(
            P(None, None, ("half", "bf")),
            P(None, ("half", "bf"), None, None),
            P(None, ("half", "bf"), None, None),
            P(None, ("half", "bf"), None, None),
            P(None, ("half", "bf"), None, None),
            P(None, ("half", "bf"), None, None),
            P(None, ("half", "bf"), None, None, None),
            P(None, ("half", "bf"), None, None, None),
            P(None, ("half", "bf"), None, None),
            P(None, ("half", "bf")),
        ),
        out_specs=P(None, None, ("half", "bf")),
        check_vma=False,
    )
```

```python
import functools

import jax
import jax.numpy as jnp
from jax import lax
from jax.experimental import pallas as pl
from jax.experimental.pallas import tpu as pltpu
from jax.sharding import PartitionSpec as P

F32 = jnp.float32
BF16 = jnp.bfloat16
MESH = pl.DeviceIdType.MESH
CORES = 2
CHIPS = 64
PART = 32
RING = 4
LEAVES = 16
RANK = 64
LEAF = 256
VECTORS = 32
CHUNKS = 2
MIX_CHUNKS = 4


def dot(left, right):
    return lax.dot_general(left, right, (((1,), (0,)), ((), ())), preferred_element_type=F32)


def dot_t(left, right):
    return lax.dot_general(left, right, (((1,), (1,)), ((), ())), preferred_element_type=F32)


def iota(shape, axis):
    return lax.broadcasted_iota(jnp.int32, shape, axis)


def farthest_first(apart):
    ways = [(0, 1.5, 2, 1.5), (4, 2.5, 2, 2.5)][apart]
    ring = (0, 1, 2, 1)
    steps = [(z, y, x) for z in range(RING) for y in range(RING) for x in range(RING)]
    return sorted(steps, key=lambda s: -(ways[s[0]] + ring[s[1]] + ring[s[2]]))


def complex_rows(by_real, by_imag):
    n = VECTORS
    return by_real[:n] - by_imag[n:], by_real[n:] + by_imag[:n]


def kernel(
    sources, coarse_in, coarse_mix_in, coarse_mix_out, coarse_out,
    fine_in, fine_mix_in, fine_mix_out, fine_out, ranks,
    out,
    x_v, ci_v, cmi_v, cmo_v, co_v, fi_v, fmi_v, fmo_v, fo_v, ranks_s,
    square, wide, ccoef, fcoef,
    c_put, c_got, c_core, f_put, f_got, f_core,
    in_sem, send_sem, recv_sem, coarse_ok, fine_ok,
):
    half = lax.axis_index("half")
    block = lax.axis_index("bf")
    core = block % CORES
    chip = block // CORES
    at_z, at_y, at_x = chip // (RING * RING), chip // RING % RING, chip % RING
    zs = [(at_z + k) % RING * (RING * RING) for k in range(RING)]
    ys = [(at_y + k) % RING * RING for k in range(RING)]
    xs = [(at_x + k) % RING for k in range(RING)]

    def chips(apart):
        return [zs[z] + ys[y] + xs[x] for z, y, x in farthest_first(apart) if apart or z + y + x]

    barrier = pltpu.get_barrier_semaphore()

    def greet(h, b):
        pl.semaphore_signal(barrier, inc=1, device_id=(h, b), device_id_type=MESH)

    per = LEAVES // CHUNKS
    deep = LEAVES * RANK // MIX_CHUNKS
    loads = {}

    def load(name, source, target):
        copy = pltpu.make_async_copy(source, target, in_sem.at[len(loads)])
        copy.start()
        loads[name] = copy

    load("ranks", ranks, ranks_s)
    for c in range(CHUNKS):
        span = pl.ds(c * per, per)
        cols = pl.ds(c * per * LEAF, per * LEAF)
        load(("x", c), sources.at[:, :, cols], x_v.at[:, :, cols])
        load(("ci", c), coarse_in.at[:, span], ci_v.at[:, span])
    for c in range(MIX_CHUNKS):
        span = pl.ds(c * deep, deep)
        load(("cmi", c), coarse_mix_in.at[:, :, span], cmi_v.at[:, :, span])
    load("fi", fine_in, fi_v)
    load("fmi", fine_mix_in, fmi_v)
    greet(half, chip * CORES + 1 - core)
    for there in chips(1):
        greet(1 - half, there * CORES + 1)
    for there in chips(0):
        greet(half, there * CORES)

    def tell(semaphore):
        to = (half, chip * CORES + 1 - core)
        pl.semaphore_signal(semaphore, inc=1, device_id=to, device_id_type=MESH)

    def hear_other_half():
        pl.semaphore_wait(barrier, CORES * CHIPS + 1)
        tell(coarse_ok)

    load("fmo", fine_mix_out, fmo_v)
    load("cmo", coarse_mix_out, cmo_v)
    load("co", coarse_out, co_v)
    load("fo", fine_out, fo_v)

    def taken(row):
        return row % (2 * PART) // 2 * 4 + (core + row // (2 * PART)) % 2 * 2 + row % 2

    square[...] = (taken(iota(square.shape, 0)) == iota(square.shape, 1)).astype(F32).astype(BF16)
    wide[...] = (taken(iota(wide.shape, 0)) == iota(wide.shape, 1) // 2).astype(F32).astype(BF16)

    lane = iota((1, 128), 1)
    low = lane < RANK

    def keep(first, second):
        return lane < jnp.where(low, first, second + RANK)

    def swapped(two):
        return pltpu.roll(two, RANK, 1)

    def column_pair(factor, which, first):
        mixed = []
        for s in (first, first + 1):
            x = x_v[:, :, s * LEAF : (s + 1) * LEAF].astype(BF16).reshape(2 * VECTORS, LEAF)
            order = (0, 1) if s == first else (1, 0)
            y = dot_t(x, jnp.concatenate([factor[order[0], s], factor[order[1], s]], axis=0))
            mine, other = y[:VECTORS], swapped(y[VECTORS:])
            mixed.append(mine + jnp.where(low == (s == first), -other, other))
        both = [jnp.where(low, mixed[0], mixed[1]), swapped(jnp.where(low, mixed[1], mixed[0]))]
        kept = keep(ranks_s[which, first], ranks_s[which, first + 1])
        return jnp.where(kept, jnp.concatenate(both, axis=0), 0.0).astype(BF16)

    loads["ranks"].wait()
    for c in range(CHUNKS):
        loads["x", c].wait()
        loads["ci", c].wait()
        for first in range(c * per, (c + 1) * per, 2):
            ccoef[:, first * RANK : (first + 2) * RANK] = column_pair(ci_v, 0, first)

    def remote(source, target, which, h, b, out=None):
        pltpu.make_async_remote_copy(
            src_ref=source, dst_ref=target, send_sem=send_sem.at[which if out is None else out], recv_sem=recv_sem.at[which],
            device_id=(h, b), device_id_type=MESH,
        ).start()

    def arrived(buffer, which):
        pltpu.make_async_copy(buffer, buffer, recv_sem.at[which]).wait()

    def sent(buffer, which):
        pltpu.make_async_copy(buffer, buffer, send_sem.at[which]).wait()

    sums = [0.0, 0.0]
    for c in range(MIX_CHUNKS):
        loads["cmi", c].wait()
        span = slice(c * deep, (c + 1) * deep)
        sums = [sums[part] + dot(ccoef[:, span], cmi_v[part, 0, span]) for part in range(2)]
    re, im = complex_rows(*sums)
    send = jnp.concatenate([re, im], axis=0)
    even = iota((1, 8 * PART), 1) % 2 == 0

    def put(target, matrix, values):
        for at in range(0, CHIPS, PART):
            step = matrix.shape[1] // PART
            part = values[:, at * step : (at + PART) * step]
            if matrix is wide:
                part = jnp.concatenate([jnp.where(even, part, 0.0), jnp.where(even, 0.0, part)], axis=0)
            rows = dot_t(matrix[...], part.astype(BF16)).astype(BF16)
            for k in range(CORES):
                target[k, at : at + PART] = rows[k * 2 * PART : (k + 1) * 2 * PART].reshape(PART, 2, 128)

    put(c_put, wide, send)

    def send_coarse(direct):
        for there in chips(1):
            if direct:
                for k, target in enumerate((c_got.at[0, chip], c_core.at[chip])):
                    to = there * CORES + (core + k) % CORES
                    remote(c_put.at[k, there], target, 2 * k, 0, to)
            else:
                remote(c_put.at[:, there], c_got.at[:, chip], 0, 1, there * CORES + core)

    @pl.when((half == 1) & (core == 1))
    def _():
        hear_other_half()

    @pl.when((half == 1) & (core == 0))
    def _():
        pl.semaphore_wait(coarse_ok, 1)

    @pl.when(half == 1)
    def _():
        send_coarse(True)

    loads["fi"].wait()
    for first in range(0, LEAVES, 2):
        fcoef[:, first * RANK : (first + 2) * RANK] = column_pair(fi_v, 2, first)
    loads["fmi"].wait()
    fine = []
    for i in range(2):
        left = fcoef[:, i * 512 : (i + 1) * 512]
        fine.extend(complex_rows(dot(left, fmi_v[0, 0, i]), dot(left, fmi_v[1, 0, i])))
    send = jnp.concatenate(fine, axis=0)
    put(f_put, square, send)
    @pl.when(core == 0)
    def _():
        pl.semaphore_wait(barrier, CORES * (CHIPS - 1) + 1)
        tell(fine_ok)

    @pl.when(core == 1)
    def _():
        pl.semaphore_wait(fine_ok, 1)

    for there in chips(0):
        remote(f_put.at[:, there], f_got.at[:, chip], 1, half, there * CORES + core)
    pltpu.make_async_copy(f_put.at[:, chip], f_got.at[:, chip], recv_sem.at[1]).start()

    @pl.when((half == 0) & (core == 1))
    def _():
        hear_other_half()

    @pl.when((half == 0) & (core == 0))
    def _():
        pl.semaphore_wait(coarse_ok, 1)

    @pl.when(half == 0)
    def _():
        send_coarse(False)

    def columns(got, landing, matrix):
        parts = []
        for at in range(0, CHIPS, PART):
            two = [got[0, at : at + PART].reshape(2 * PART, 128), landing[at : at + PART].reshape(2 * PART, 128)]
            parts.append(dot(jnp.concatenate(two, axis=0).T, matrix[...]))
        if matrix is wide:
            parts = [jnp.where(even, part[:64], part[64:]) for part in parts]
        return jnp.concatenate(parts, axis=1).astype(BF16)

    def row_leaves(pair, which, leaf, factor, add):
        for n in range(2):
            first = leaf + 2 * n
            kept = keep(ranks_s[which, first], ranks_s[which, first + 1])
            re, im = [jnp.where(kept, part[:, 128 * n : 128 * n + 128], 0.0) for part in pair]
            re_other, im_other = swapped(re), swapped(im)
            for s in (first, first + 1):
                if s == first:
                    rows = [jnp.where(low, re, -im_other), jnp.where(low, im, re_other)]
                    w = jnp.concatenate([factor[0, s], factor[1, s]], axis=0)
                else:
                    rows = [jnp.where(low, -im_other, re), jnp.where(low, re_other, im)]
                    w = jnp.concatenate([factor[1, s], factor[0, s]], axis=0)
                y = dot(jnp.concatenate(rows, axis=0).astype(BF16), w).reshape(2, VECTORS, LEAF)
                cols = slice(s * LEAF, (s + 1) * LEAF)
                out[:, :, cols] = out[:, :, cols] + y if add else y

    arrived(f_got, 1)
    remote(f_got.at[1], f_core, 3, half, chip * CORES + 1 - core)
    arrived(f_core, 3)
    got = columns(f_got, f_core, square)
    loads["fmo"].wait()
    loads["fo"].wait()
    for i in range(2):
        left = got[i * 64 : i * 64 + 64]
        for at in range(0, 512, 256):
            pair = complex_rows(
                dot(left, fmo_v[0, 0, i, :, at : at + 256]), dot(left, fmo_v[1, 0, i, :, at : at + 256])
            )
            row_leaves(pair, 3, ((1 - i) * 512 + at) // RANK, fo_v, False)

    @pl.when(half == 0)
    def _():
        arrived(c_got.at[0], 0)

    @pl.when(half == 1)
    def _():
        arrived(c_got, 0)
        remote(c_got.at[1], c_core, 2, 1, chip * CORES + 1 - core, 4)

    arrived(c_core, 2)
    left = columns(c_got, c_core, wide)
    loads["cmo"].wait()
    loads["co"].wait()
    for at in range(0, 1024, 256):
        pair = complex_rows(dot(left, cmo_v[0, 0, :, at : at + 256]), dot(left, cmo_v[1, 0, :, at : at + 256]))
        row_leaves(pair, 1, at // RANK, co_v, True)

    @pl.when(half == 0)
    def _():
        sent(c_put, 0)

    @pl.when(half == 1)
    def _():
        sent(c_put.at[0], 0)
        sent(c_put.at[1], 2)
        sent(c_core, 4)

    sent(f_put.at[:, pl.ds(0, CHIPS - 1)], 1)
    sent(f_core, 3)


def local(*args):
    hbm = pl.BlockSpec(memory_space=pltpu.HBM)
    shapes = [a.shape for a in args]
    vmem = pltpu.VMEM
    return pl.pallas_call(
        kernel,
        out_shape=jax.ShapeDtypeStruct(shapes[0], F32),
        in_specs=[hbm] * len(args),
        out_specs=pl.BlockSpec(memory_space=pltpu.VMEM),
        scratch_shapes=[
            vmem(shapes[0], F32),
            *[vmem(s, BF16) for s in shapes[1:9]],
            pltpu.SMEM(shapes[9], jnp.int32),
            vmem((4 * PART, 4 * PART), BF16),
            vmem((4 * PART, 8 * PART), BF16),
            vmem((64, 1024), BF16),
            vmem((64, 1024), BF16),
            *[vmem(s, BF16) for s in [(CORES, CHIPS, 2, 128), (CORES, CHIPS, 2, 128), (CHIPS, 2, 128)] * 2],
            pltpu.SemaphoreType.DMA((1 + 2 * CHUNKS + MIX_CHUNKS + 6,)),
            pltpu.SemaphoreType.DMA((5,)),
            pltpu.SemaphoreType.DMA((4,)),
            pltpu.SemaphoreType.REGULAR,
            pltpu.SemaphoreType.REGULAR,
        ],
        compiler_params=pltpu.CompilerParams(
            collective_id=0, has_side_effects=True, vmem_limit_bytes=40 * 1024 * 1024
        ),
        cost_estimate=pl.CostEstimate(flops=672 * 10**6, bytes_accessed=12 * 2**20, transcendentals=0),
    )(*[pltpu.with_memory_space_constraint(a, pltpu.HBM) for a in args])


def solution(mesh):
    return jax.shard_map(
        local,
        mesh=mesh,
        in_specs=(
            P(None, None, ("half", "bf")),
            P(None, ("half", "bf"), None, None),
            P(None, ("half", "bf"), None, None),
            P(None, ("half", "bf"), None, None),
            P(None, ("half", "bf"), None, None),
            P(None, ("half", "bf"), None, None),
            P(None, ("half", "bf"), None, None, None),
            P(None, ("half", "bf"), None, None, None),
            P(None, ("half", "bf"), None, None),
            P(None, ("half", "bf")),
        ),
        out_specs=P(None, None, ("half", "bf")),
        check_vma=False,
    )
```
